768 devices in a mesh: dp: 96 (over y, z), shard: 8 (over x, core).
Axes of the slice: x: 4, y: 8, z: 12, core: 2. Of those that a mesh axis runs over, the one named last changes fastest.
Arguments:
- grad_partials: bfloat16 [96, 8, 1536, 512], P('dp', 'shard')
Outputs:
- update_blocks: float32 [8, 1536, 512], P('shard', 'dp')
All inputs are finite; a program needn't handle non-finite values.
Results may differ from the reference program's by a relative error of at most 0.0059.
Values may be sent and summed in bfloat16 or wider, within the bound.
A program may use at most 32 MiB of HBM per device.

```python
import math
import jax
import jax.numpy as jnp
from jax import lax

BS = 512
KB = 3
ITERS = 2
NB = 24
N_DP = 96
N_SHARD = 8


def draw_grad_partials(key, part):
    key = jax.random.fold_in(key, 11)
    key_noise, key_rows, key_cols = jax.random.split(key, 3)
    columns = NB // KB
    shape = (N_DP, columns, KB * BS, BS)
    row_scale = jnp.exp(jax.random.uniform(key_rows, (columns, KB * BS), jnp.float32, 0.0, math.log(10.0)))
    col_scale = jnp.exp(jax.random.uniform(key_cols, (BS,), jnp.float32, 0.0, math.log(10.0)))
    column_ramp = 1.0 + 2.0 * jnp.arange(columns, dtype=jnp.float32) / max(columns - 1, 1)
    noise = jnp.clip(jax.random.normal(key_noise, shape, jnp.float32), -6.0, 6.0)
    scaled = 0.05 * noise * column_ramp[None, :, None, None] * row_scale[None, :, :, None] * col_scale
    return scaled.astype(jnp.bfloat16)


def setup_inputs(seed: int = 0) -> dict:
    arg_keys = jax.random.split(jax.random.key(seed), 2)
    grad_partials = draw_grad_partials(jax.random.fold_in(arg_keys[1], 71), 0)
    return {"grad_partials": grad_partials}


ridge = 0.1
target_rms = 0.5

def matmul_high(left, right):
    return jnp.dot(left, right, precision=lax.Precision.HIGHEST, preferred_element_type=jnp.float32)

def newton_root(statistic):
    identity = jnp.eye(statistic.shape[0], dtype=jnp.float32)
    norm_scale = jnp.sqrt(jnp.sum(statistic * statistic))
    moment = statistic / norm_scale
    start_scale = norm_scale ** (-0.25)
    iterate = identity * start_scale
    for iteration in range(ITERS):
        factor = (5.0 * identity - moment) * 0.25
        if iteration == 0:
            iterate = factor * start_scale
        else:
            iterate = matmul_high(iterate, factor)
        if iteration + 1 < ITERS:
            square = matmul_high(factor, factor)
            fourth = matmul_high(square, square)
            moment = matmul_high(fourth, moment)
    return iterate.astype(jnp.bfloat16)

def precondition(block):
    identity = jnp.eye(BS, dtype=jnp.float32)
    left = jnp.dot(block, block.T, preferred_element_type=jnp.float32) / BS + ridge * identity
    right = jnp.dot(block.T, block, preferred_element_type=jnp.float32) / BS + ridge * identity
    left_root = newton_root(left)
    right_root = newton_root(right)
    hidden = jnp.dot(left_root, block, preferred_element_type=jnp.float32).astype(jnp.bfloat16)
    return jnp.dot(hidden, right_root, preferred_element_type=jnp.float32)

def reference(grad_partials):

    def accumulate(index, column_acc):
        return column_acc + grad_partials[index].astype(jnp.float32)
    column_sum = lax.fori_loop(0, N_DP, accumulate, jnp.zeros((N_SHARD, KB * BS, BS), jnp.float32))
    sumsq = jnp.sum(column_sum * column_sum)
    clip_factor = target_rms * BS * math.sqrt(NB) / jnp.sqrt(sumsq)
    clipped = (column_sum * clip_factor).astype(jnp.bfloat16)
    blocks = clipped.reshape(NB, BS, BS)
    result = lax.map(precondition, blocks)
    return result.reshape(N_SHARD, KB * BS, BS)
```

```python
import functools
import math

import jax
import jax.numpy as jnp
from jax import lax
from jax.experimental import pallas as pl
from jax.experimental.pallas import tpu as pltpu
from jax.sharding import PartitionSpec as P

MESH = pl.DeviceIdType.MESH
NY, NZ, NS = 8, 12, 8
PARTS = 4
PER_BLOCK = 32
BLOCKS = 3
ROOTS = BLOCKS * NS
RIDGE = 0.1
TARGET_RMS = 0.5
F32, BF16 = jnp.float32, jnp.bfloat16


def series():
    coefs = [25.0 / 16.0, -5.0 / 16.0, 0.0, 0.0, 0.0, 0.0, 0.0]
    for power in range(6):
        coefs[power + 1] -= math.comb(5, power) * 5.0 ** (5 - power) * (-1.0) ** power / 4096.0
    return coefs


def shifted(beta, gamma):
    coefs = series()
    out = []
    scale = jnp.ones_like(beta)
    for j in range(7):
        total = jnp.zeros_like(beta)
        for i in range(6, j - 1, -1):
            total = total * gamma + coefs[i] * math.comb(i, j)
        out.append(total * scale)
        scale = scale * beta
    return out


def root_of(block, shard):
    row = 1 + 2 * block + block // 2
    return row * NZ + lax.rem(shard, 2)


def dot(a, b, dims):
    return lax.dot_general(a, b, (dims, ((), ())), preferred_element_type=F32)


NN = ((1,), (0,))
NT = ((1,), (1,))
TN = ((0,), (0,))


def kernel(
    g_ref, out_ref,
    loc, rbuf, lbuf, rsend, lsend, zsend, own, zbuf, piece, sq, gath, gsq, tot, xbuf, upd, land,
    loc_sem, rs_sem, rr_sem, ls_sem, lr_sem, zs_sem, zr_sem, gs_sem, gr_sem, qs_sem, qr_sem,
    xs_sem, xr_sem, us_sem, ur_sem,
):
    i = lax.axis_index("dp")
    s = lax.axis_index("shard")
    y, z = i // NZ, lax.rem(i, NZ)
    block, mine = i // PER_BLOCK, lax.rem(i, PER_BLOCK)
    root = root_of(block, s)
    is_root = i == root
    here = block * NS + s

    def yy(d):
        return lax.rem(y + d + NY, NY)

    def zz(d):
        return lax.rem(z + d + NZ, NZ)

    def remote(src, dst, ssem, rsem, dev):
        return pltpu.make_async_remote_copy(
            src_ref=src, dst_ref=dst, send_sem=ssem, recv_sem=rsem,
            device_id=dev, device_id_type=MESH,
        )

    local = pltpu.make_async_copy(g_ref, loc, loc_sem)
    local.start()

    barrier = pltpu.get_barrier_semaphore()

    def greet(dp, shard):
        pl.semaphore_signal(barrier, inc=1, device_id=(dp, shard), device_id_type=MESH)

    up, down = yy(1) * NZ + z, yy(-1) * NZ + z
    greet(up, s)
    greet(down, s)
    for d in range(1, NZ):
        greet(y * NZ + zz(d), s)

    @pl.when(is_root)
    def _():
        @pl.loop(1, PER_BLOCK)
        def _(d):
            greet(block * PER_BLOCK + lax.rem(mine + d, PER_BLOCK), s)

        @pl.loop(1, ROOTS)
        def _(d):
            q = lax.rem(here + d, ROOTS)
            greet(root_of(q // NS, lax.rem(q, NS)), lax.rem(q, NS))

        pl.semaphore_wait(barrier, 2 + NZ - 1 + PER_BLOCK - 1 + ROOTS - 1)

    @pl.when(jnp.logical_not(is_root))
    def _():
        greet(root, s)
        pl.semaphore_wait(barrier, 2 + NZ - 1 + 1)

    def count(way, j):
        return 4 if (j < PARTS // 2) == (way > 0) else 3

    tables = {1: (rbuf, rsend, rs_sem, rr_sem), -1: (lbuf, lsend, ls_sem, lr_sem)}
    started = []

    def ring(way, j, t):
        buf, sends, ssem, rsem = tables[way]
        src = g_ref.at[yy(way * count(way, j)), :, j] if t == 0 else sends.at[j, t - 1]
        return remote(src, buf.at[j, t], ssem.at[j, t], rsem.at[j, t], (up if way > 0 else down, s))

    for t in range(4):
        for j in range(PARTS):
            for way in (1, -1):
                if t >= count(way, j):
                    continue
                if t > 0:
                    if t == 1 and j == 0 and way == 1:
                        local.wait()
                    buf, sends, _, _ = tables[way]
                    ring(way, j, t - 1).wait_recv()
                    chunk = yy(way * (count(way, j) - t))
                    sends[j, t - 1] = (
                        loc[chunk, :, j].astype(F32) + buf[j, t - 1].astype(F32)
                    ).astype(BF16)
                copy = ring(way, j, t)
                copy.start()
                started.append(copy)

    def across(j, a):
        to = 4 * a + j
        return to, remote(
            zsend.at[j, a], zbuf.at[lax.rem(to - z + NZ, NZ)], zs_sem.at[to],
            zr_sem.at[lax.rem(to - z + NZ, NZ)], (y * NZ + to, s),
        )

    for j in range(PARTS):
        ring(1, j, count(1, j) - 1).wait_recv()
        ring(-1, j, count(-1, j) - 1).wait_recv()
        total = (
            loc[y, :, j].astype(F32)
            + rbuf[j, count(1, j) - 1].astype(F32)
            + lbuf[j, count(-1, j) - 1].astype(F32)
        )
        zsend[j] = total.astype(BF16)
        for a in range(3):
            to, copy = across(j, a)

            @pl.when(z != to)
            def _():
                copy.start()

            @pl.when(z == to)
            def _():
                own[...] = total[a]

    rows = own[...]
    for d in range(1, NZ):
        remote(zsend.at[0, 0], zbuf.at[d], zs_sem.at[0], zr_sem.at[d], (up, s)).wait_recv()
        rows = rows + zbuf[d].astype(F32)

    piece[...] = rows.astype(BF16)
    squares = rows * rows
    folded = squares[0:8] + squares[8:16]
    sq[...] = folded[:, 0:128] + folded[:, 128:256] + folded[:, 256:384] + folded[:, 384:512]

    def to_root(slot):
        return (
            remote(piece, gath.at[slot], gs_sem, gr_sem.at[slot], (root, s)),
            remote(sq, gsq.at[slot], qs_sem, qr_sem.at[slot], (root, s)),
        )

    @pl.when(jnp.logical_not(is_root))
    def _():
        for copy in to_root(mine):
            copy.start()

    def from_root(m):
        return remote(
            upd.at[m], land, us_sem.at[m], ur_sem, (block * PER_BLOCK + m, s)
        )

    @pl.when(is_root)
    def _():
        gath[mine] = piece[...]
        gsq[mine] = sq[...]

        @pl.loop(1, PER_BLOCK)
        def _(d):
            for copy in to_root(lax.rem(mine + d, PER_BLOCK)):
                copy.wait_recv()

        block_sq = jnp.sum(gsq[...], axis=0)
        tot[...] = block_sq

        def to_other(q, slot):
            return remote(
                tot, xbuf.at[slot], xs_sem.at[q], xr_sem.at[slot],
                (root_of(q // NS, lax.rem(q, NS)), lax.rem(q, NS)),
            )

        @pl.loop(1, ROOTS)
        def _(d):
            to_other(lax.rem(here + d, ROOTS), here).start()

        width = 16 * PER_BLOCK
        grad = gath[...].reshape(width, width)
        fb = jnp.sum(block_sq, keepdims=True)
        inverse = jnp.where(fb > 0.0, 1.0 / fb, 0.0)
        left = dot(grad, grad, NT) * inverse
        right = dot(grad, grad, TN) * inverse
        eye = lax.broadcasted_iota(jnp.int32, (width, width), 0) == lax.broadcasted_iota(
            jnp.int32, (width, width), 1
        )
        trace = jnp.sum(jnp.where(eye, left, 0.0), keepdims=True)
        norm2 = jnp.sum(left * left, keepdims=True)

        def powers(n):
            nb = n.astype(BF16)
            q = dot(nb, nb, NN)
            return q, dot(nb, q.astype(BF16), NN)

        left2, left3 = powers(left)
        right2, right3 = powers(right)

        xbuf[here] = block_sq

        @pl.loop(1, ROOTS)
        def _(d):
            q = lax.rem(here + d, ROOTS)
            to_other(q, q).wait_recv()

        sumsq = jnp.sum(jnp.sum(xbuf[...], axis=0), keepdims=True)
        limit = TARGET_RMS * width * math.sqrt(ROOTS)
        clip = limit / jnp.sqrt(sumsq)
        kappa = (limit * limit / width) * (fb / sumsq)
        c2 = kappa * kappa * norm2 + (2.0 * RIDGE) * kappa * trace + RIDGE * RIDGE * width
        c = jnp.sqrt(c2)
        start = lax.rsqrt(jnp.sqrt(c))
        coefs = [v * start for v in shifted(kappa / c, RIDGE / c)]

        def finish(n, q, k):
            high = (coefs[4] * n + coefs[5] * q + coefs[6] * k).astype(BF16)
            low = coefs[1] * n + coefs[2] * q + coefs[3] * k + jnp.where(eye, coefs[0], 0.0)
            return (low + dot(k.astype(BF16), high, NN)).astype(BF16)

        left_root = finish(left, left2, left3)
        hidden = (clip * dot(left_root, grad, NN)).astype(BF16)
        right_root = finish(right, right2, right3)
        upd[...] = dot(hidden, right_root, NN).reshape(PER_BLOCK, 16, width)

        @pl.loop(1, PER_BLOCK)
        def _(d):
            from_root(lax.rem(mine + d, PER_BLOCK)).start()

        out_ref[...] = upd[mine]

        @pl.loop(1, PER_BLOCK)
        def _(d):
            from_root(lax.rem(mine + d, PER_BLOCK)).wait_send()

        @pl.loop(1, ROOTS)
        def _(d):
            to_other(lax.rem(here + d, ROOTS), here).wait_send()

    @pl.when(jnp.logical_not(is_root))
    def _():
        for copy in to_root(mine):
            copy.wait_send()

    for copy in started:
        copy.wait_send()
    for j in range(PARTS):
        for a in range(3):
            to, copy = across(j, a)

            @pl.when(z != to)
            def _():
                copy.wait_send()

    @pl.when(jnp.logical_not(is_root))
    def _():
        from_root(mine).wait_recv()
        out_ref[...] = land[...]


def body(grad_partials):
    width = grad_partials.shape[-1]
    g = grad_partials.reshape(NY, 3, PARTS, 16, width)
    dma = pltpu.SemaphoreType.DMA
    out = pl.pallas_call(
        kernel,
        out_shape=jax.ShapeDtypeStruct((16, width), F32),
        in_specs=[pl.BlockSpec(memory_space=pl.ANY)],
        out_specs=pl.BlockSpec(memory_space=pltpu.VMEM),
        scratch_shapes=[
            pltpu.VMEM((NY, 3, PARTS, 16, width), BF16),
            pltpu.VMEM((PARTS, 4, 3, 16, width), BF16),
            pltpu.VMEM((PARTS, 4, 3, 16, width), BF16),
            pltpu.VMEM((PARTS, 3, 3, 16, width), BF16),
            pltpu.VMEM((PARTS, 3, 3, 16, width), BF16),
            pltpu.VMEM((PARTS, 3, 16, width), BF16),
            pltpu.VMEM((16, width), F32),
            pltpu.VMEM((NZ, 16, width), BF16),
            pltpu.VMEM((16, width), BF16),
            pltpu.VMEM((8, 128), F32),
            pltpu.VMEM((PER_BLOCK, 16, width), BF16),
            pltpu.VMEM((PER_BLOCK, 8, 128), F32),
            pltpu.VMEM((8, 128), F32),
            pltpu.VMEM((ROOTS, 8, 128), F32),
            pltpu.VMEM((PER_BLOCK, 16, width), F32),
            pltpu.VMEM((16, width), F32),
            dma,
            dma((PARTS, 4)), dma((PARTS, 4)), dma((PARTS, 4)), dma((PARTS, 4)),
            dma((NZ,)), dma((NZ,)),
            dma, dma((PER_BLOCK,)), dma, dma((PER_BLOCK,)),
            dma((ROOTS,)), dma((ROOTS,)), dma((PER_BLOCK,)), dma,
        ],
        compiler_params=pltpu.CompilerParams(
            collective_id=0, has_side_effects=True, vmem_limit_bytes=48 * 2**20
        ),
    )(g)
    return out[None]


def solution(mesh):
    placed = (P("dp", "shard", None, None),)
    return jax.shard_map(
        body, mesh=mesh, in_specs=placed, out_specs=P("shard", "dp", None), check_vma=False
    )
```

```python
import functools
import math

import jax
import jax.numpy as jnp
from jax import lax
from jax.experimental import pallas as pl
from jax.experimental.pallas import tpu as pltpu
from jax.sharding import PartitionSpec as P

MESH = pl.DeviceIdType.MESH
NY, NZ, NS = 8, 12, 8
PARTS = 4
PER_BLOCK = 32
BLOCKS = 3
ROOTS = BLOCKS * NS
RIDGE = 0.1
TARGET_RMS = 0.5
F32, BF16 = jnp.float32, jnp.bfloat16


def series():
    coefs = [25.0 / 16.0, -5.0 / 16.0, 0.0, 0.0, 0.0, 0.0, 0.0]
    for power in range(6):
        coefs[power + 1] -= math.comb(5, power) * 5.0 ** (5 - power) * (-1.0) ** power / 4096.0
    return coefs


def shifted(beta, gamma):
    coefs = series()
    out = []
    scale = jnp.ones_like(beta)
    for j in range(7):
        total = jnp.zeros_like(beta)
        for i in range(6, j - 1, -1):
            total = total * gamma + coefs[i] * math.comb(i, j)
        out.append(total * scale)
        scale = scale * beta
    return out


def root_of(block, shard):
    row = 1 + 2 * block + block // 2
    return row * NZ + NZ - 1 - 8 * lax.rem(shard, 2)


def dot(a, b, dims):
    return lax.dot_general(a, b, (dims, ((), ())), preferred_element_type=F32)


NN = ((1,), (0,))
NT = ((1,), (1,))
TN = ((0,), (0,))


def kernel(
    g_ref, out_ref,
    loc, rbuf, lbuf, rsend, lsend, zsend, own, zbuf, piece, sq, gath, peers, line, lines, upd, land,
    loc_sem, rs_sem, rr_sem, ls_sem, lr_sem, zs_sem, zr_sem, gs_sem, gr_sem, ps_sem, pr_sem,
    ts_sem, tr_sem, us_sem, ur_sem, known,
):
    i = lax.axis_index("dp")
    s = lax.axis_index("shard")
    y, z = i // NZ, lax.rem(i, NZ)
    block, mine = i // PER_BLOCK, lax.rem(i, PER_BLOCK)
    root = root_of(block, s)
    is_root = i == root

    def yy(d):
        return lax.rem(y + d + NY, NY)

    def zz(d):
        return lax.rem(z + d + NZ, NZ)

    def remote(src, dst, ssem, rsem, dev):
        return pltpu.make_async_remote_copy(
            src_ref=src, dst_ref=dst, send_sem=ssem, recv_sem=rsem,
            device_id=dev, device_id_type=MESH,
        )

    local = pltpu.make_async_copy(g_ref, loc, loc_sem)
    local.start()

    barrier = pltpu.get_barrier_semaphore()

    def greet(dp, shard):
        pl.semaphore_signal(barrier, inc=1, device_id=(dp, shard), device_id_type=MESH)

    up, down = yy(1) * NZ + z, yy(-1) * NZ + z
    greet(up, s)
    greet(down, s)
    greet(y * NZ + zz(1), s)
    greet(y * NZ + zz(-1), s)
    for d in range(1, NS):
        greet(i, lax.rem(s + d, NS))
    pl.semaphore_wait(barrier, 4 + NS - 1)

    def tell(stage):
        for side, sign in ((0, 1), (1, -1)):
            pl.semaphore_signal(
                known.at[stage, side], inc=1,
                device_id=(y * NZ + zz(sign * 2**stage), s), device_id_type=MESH,
            )

    def hear(stage):
        pl.semaphore_wait(known.at[stage, 0], 1)
        pl.semaphore_wait(known.at[stage, 1], 1)

    def count(way, j):
        return 4 if (j < PARTS // 2) == (way > 0) else 3

    tables = {1: (rbuf, rsend, rs_sem, rr_sem), -1: (lbuf, lsend, ls_sem, lr_sem)}
    started = []

    def ring(way, j, t):
        buf, sends, ssem, rsem = tables[way]
        src = g_ref.at[yy(way * count(way, j)), :, j] if t == 0 else sends.at[j, t - 1]
        return remote(src, buf.at[j, t], ssem.at[j, t], rsem.at[j, t], (up if way > 0 else down, s))

    for t in range(4):
        if t > 1:
            hear(t - 2)
        if t > 0:
            tell(t - 1)
        for j in range(PARTS):
            for way in (1, -1):
                if t >= count(way, j):
                    continue
                if t > 0:
                    if t == 1 and j == 0 and way == 1:
                        local.wait()
                    buf, sends, _, _ = tables[way]
                    ring(way, j, t - 1).wait_recv()
                    chunk = yy(way * (count(way, j) - t))
                    sends[j, t - 1] = (
                        loc[chunk, :, j].astype(F32) + buf[j, t - 1].astype(F32)
                    ).astype(BF16)
                copy = ring(way, j, t)
                copy.start()
                started.append(copy)

    def across(j, a):
        to = 4 * a + j
        return to, remote(
            zsend.at[j, a], zbuf.at[lax.rem(to - z + NZ, NZ)], zs_sem.at[to],
            zr_sem.at[lax.rem(to - z + NZ, NZ)], (y * NZ + to, s),
        )

    hear(2)
    for j in range(PARTS):
        ring(1, j, count(1, j) - 1).wait_recv()
        ring(-1, j, count(-1, j) - 1).wait_recv()
        total = (
            loc[y, :, j].astype(F32)
            + rbuf[j, count(1, j) - 1].astype(F32)
            + lbuf[j, count(-1, j) - 1].astype(F32)
        )
        zsend[j] = total.astype(BF16)
        for a in range(3):
            to, copy = across(j, a)

            @pl.when(z != to)
            def _():
                copy.start()

            @pl.when(z == to)
            def _():
                own[...] = total[a]

    rows = own[...]
    for d in range(1, NZ):
        remote(zsend.at[0, 0], zbuf.at[d], zs_sem.at[0], zr_sem.at[d], (up, s)).wait_recv()
        rows = rows + zbuf[d].astype(F32)

    piece[...] = rows.astype(BF16)
    squares = rows * rows
    folded = squares[0:8] + squares[8:16]
    sq[...] = folded[:, 0:128] + folded[:, 128:256] + folded[:, 256:384] + folded[:, 384:512]

    def to_peer(d):
        return remote(sq, peers.at[d], ps_sem.at[d], pr_sem.at[d], (i, lax.rem(s + d, NS)))

    for d in range(1, NS):
        to_peer(d).start()

    def to_root(slot):
        return remote(piece, gath.at[slot], gs_sem, gr_sem, (root, s))

    @pl.when(jnp.logical_not(is_root))
    def _():
        to_root(mine).start()

    row_sq = sq[...]
    for d in range(1, NS):
        to_peer(d).wait_recv()
        row_sq = row_sq + peers[d]
    line[...] = row_sq

    def to_column(b, slot):
        return remote(line, lines.at[slot], ts_sem.at[b], tr_sem, (root_of(b, s), s))

    for b in range(BLOCKS):
        copy = to_column(b, i)

        @pl.when(i != root_of(b, s))
        def _():
            copy.start()

    def from_root(m):
        return remote(
            upd.at[m], land, us_sem.at[m], ur_sem, (block * PER_BLOCK + m, s)
        )

    @pl.when(is_root)
    def _():
        gath[mine] = piece[...]
        lines[i] = row_sq
        remote(
            gath.at[pl.ds(0, PER_BLOCK - 1)], gath.at[pl.ds(0, PER_BLOCK - 1)], gs_sem, gr_sem, (up, s)
        ).wait_recv()

        width = 16 * PER_BLOCK
        grad = gath[...].reshape(width, width)
        wide = grad.astype(F32)
        fb = jnp.sum(wide * wide, keepdims=True)
        inverse = jnp.where(fb > 0.0, 1.0 / fb, 0.0)
        left = dot(grad, grad, NT) * inverse
        right = dot(grad, grad, TN) * inverse
        eye = lax.broadcasted_iota(jnp.int32, (width, width), 0) == lax.broadcasted_iota(
            jnp.int32, (width, width), 1
        )
        trace = jnp.where(fb > 0.0, 1.0, 0.0)
        norm2 = jnp.sum(left * left, keepdims=True)

        def powers(n):
            nb = n.astype(BF16)
            q = dot(nb, nb, NN)
            return q, dot(nb, q.astype(BF16), NN)

        left2, left3 = powers(left)
        right2, right3 = powers(right)

        others = NY * NZ - 1
        remote(
            lines.at[pl.ds(0, others)], lines.at[pl.ds(0, others)], gs_sem, tr_sem, (up, s)
        ).wait_recv()

        sumsq = jnp.sum(jnp.sum(lines[...], axis=0), keepdims=True)
        limit = TARGET_RMS * width * math.sqrt(ROOTS)
        clip = limit / jnp.sqrt(sumsq)
        kappa = (limit * limit / width) * (fb / sumsq)
        c2 = kappa * kappa * norm2 + (2.0 * RIDGE) * kappa * trace + RIDGE * RIDGE * width
        c = jnp.sqrt(c2)
        start = lax.rsqrt(jnp.sqrt(c))
        coefs = [v * start for v in shifted(kappa / c, RIDGE / c)]

        def finish(n, q, k):
            high = (coefs[4] * n + coefs[5] * q + coefs[6] * k).astype(BF16)
            low = coefs[1] * n + coefs[2] * q + coefs[3] * k + jnp.where(eye, coefs[0], 0.0)
            return (low + dot(k.astype(BF16), high, NN)).astype(BF16)

        left_root = finish(left, left2, left3)
        hidden = (clip * dot(left_root, grad, NN)).astype(BF16)
        right_root = finish(right, right2, right3)
        upd[...] = dot(hidden, right_root, NN).reshape(PER_BLOCK, 16, width)

        first = 5 * block // 2

        @pl.loop(0, 4 * NZ)
        def _(k):
            m = (first + lax.rem(k, 4)) * NZ + k // 4 - block * PER_BLOCK

            @pl.when(jnp.logical_and(jnp.logical_and(m >= 0, m < PER_BLOCK), m != mine))
            def _():
                from_root(m).start()

        out_ref[...] = upd[mine]

        @pl.loop(1, PER_BLOCK)
        def _(d):
            from_root(lax.rem(mine + d, PER_BLOCK)).wait_send()

    @pl.when(jnp.logical_not(is_root))
    def _():
        to_root(mine).wait_send()

    for d in range(1, NS):
        to_peer(d).wait_send()
    for b in range(BLOCKS):
        copy = to_column(b, i)

        @pl.when(i != root_of(b, s))
        def _():
            copy.wait_send()

    for copy in started:
        copy.wait_send()
    for j in range(PARTS):
        for a in range(3):
            to, copy = across(j, a)

            @pl.when(z != to)
            def _():
                copy.wait_send()

    @pl.when(jnp.logical_not(is_root))
    def _():
        from_root(mine).wait_recv()
        out_ref[...] = land[...]


def body(grad_partials):
    width = grad_partials.shape[-1]
    g = grad_partials.reshape(NY, 3, PARTS, 16, width)
    dma = pltpu.SemaphoreType.DMA
    out = pl.pallas_call(
        kernel,
        out_shape=jax.ShapeDtypeStruct((16, width), F32),
        in_specs=[pl.BlockSpec(memory_space=pl.ANY)],
        out_specs=pl.BlockSpec(memory_space=pltpu.VMEM),
        scratch_shapes=[
            pltpu.VMEM((NY, 3, PARTS, 16, width), BF16),
            pltpu.VMEM((PARTS, 4, 3, 16, width), BF16),
            pltpu.VMEM((PARTS, 4, 3, 16, width), BF16),
            pltpu.VMEM((PARTS, 3, 3, 16, width), BF16),
            pltpu.VMEM((PARTS, 3, 3, 16, width), BF16),
            pltpu.VMEM((PARTS, 3, 16, width), BF16),
            pltpu.VMEM((16, width), F32),
            pltpu.VMEM((NZ, 16, width), BF16),
            pltpu.VMEM((16, width), BF16),
            pltpu.VMEM((8, 128), F32),
            pltpu.VMEM((PER_BLOCK, 16, width), BF16),
            pltpu.VMEM((NS, 8, 128), F32),
            pltpu.VMEM((8, 128), F32),
            pltpu.VMEM((NY * NZ, 8, 128), F32),
            pltpu.VMEM((PER_BLOCK, 16, width), F32),
            pltpu.VMEM((16, width), F32),
            dma,
            dma((PARTS, 4)), dma((PARTS, 4)), dma((PARTS, 4)), dma((PARTS, 4)),
            dma((NZ,)), dma((NZ,)),
            dma, dma, dma((NS,)), dma((NS,)),
            dma((BLOCKS,)), dma, dma((PER_BLOCK,)), dma,
            pltpu.SemaphoreType.REGULAR((3, 2)),
        ],
        compiler_params=pltpu.CompilerParams(
            collective_id=0, has_side_effects=True, vmem_limit_bytes=48 * 2**20
        ),
    )(g)
    return out[None]


def solution(mesh):
    placed = (P("dp", "shard", None, None),)
    return jax.shard_map(
        body, mesh=mesh, in_specs=placed, out_specs=P("shard", "dp", None), check_vma=False
    )
```

```python
import functools
import math

import jax
import jax.numpy as jnp
from jax import lax
from jax.experimental import pallas as pl
from jax.experimental.pallas import tpu as pltpu
from jax.sharding import PartitionSpec as P

MESH = pl.DeviceIdType.MESH
NY, NZ, NS = 8, 12, 8
PARTS = 4
NARROW = 128
PER_BLOCK = 32
BLOCKS = 3
SPANS = 3
RIDGE = 0.1
TARGET_RMS = 0.5
F32, BF16 = jnp.float32, jnp.bfloat16


def series():
    coefs = [25.0 / 16.0, -5.0 / 16.0, 0.0, 0.0, 0.0, 0.0, 0.0]
    for power in range(6):
        coefs[power + 1] -= math.comb(5, power) * 5.0 ** (5 - power) * (-1.0) ** power / 4096.0
    return coefs


def shifted(beta, gamma):
    coefs = series()
    out = []
    scale = jnp.ones_like(beta)
    for j in range(7):
        total = jnp.zeros_like(beta)
        for i in range(6, j - 1, -1):
            total = total * gamma + coefs[i] * math.comb(i, j)
        out.append(total * scale)
        scale = scale * beta
    return out


def root_of(block, shard, k):
    row = 1 + 2 * block + block // 2
    return row * NZ + lax.rem(NZ - 1 + 2 * lax.rem(shard, 2) + 4 * k, NZ)


def dot(a, b, dims):
    return lax.dot_general(a, b, (dims, ((), ())), preferred_element_type=F32)


NN = ((1,), (0,))
TN = ((0,), (0,))


def kernel(
    g_ref, out_ref,
    loc, pick, rbuf, lbuf, rsend, lsend, zsend, own, zbuf, araw, asum, afin, asend, abuf, piece, sq, gath, peers, line, lines, upd, land,
    loc_sem, rs_sem, rr_sem, ls_sem, lr_sem, zs_sem, zr_sem, gs_sem, gr_sem, ps_sem, pr_sem,
    ts_sem, tr_sem, us_sem, ur_sem, known, along,
    as_sem, ar_sem, bs_sem, br_sem, cs_sem, cr_sem,
):
    i = lax.axis_index("dp")
    s = lax.axis_index("shard")
    y, z = i // NZ, lax.rem(i, NZ)
    block, mine = i // PER_BLOCK, lax.rem(i, PER_BLOCK)
    ahead = lax.rem(z + NZ + 2 - 2 * lax.rem(s, 2), NZ)
    span = ahead // 4
    is_root = functools.reduce(jnp.logical_or, [i == root_of(block, s, k) for k in range(SPANS)])

    def yy(d):
        return lax.rem(y + d + NY, NY)

    def zz(d):
        return lax.rem(z + d + NZ, NZ)

    def remote(src, dst, ssem, rsem, dev):
        return pltpu.make_async_remote_copy(
            src_ref=src, dst_ref=dst, send_sem=ssem, recv_sem=rsem,
            device_id=dev, device_id_type=MESH,
        )

    local = pltpu.make_async_copy(g_ref, loc, loc_sem)
    local.start()

    barrier = pltpu.get_barrier_semaphore()

    def greet(dp, shard):
        pl.semaphore_signal(barrier, inc=1, device_id=(dp, shard), device_id_type=MESH)

    up, down = yy(1) * NZ + z, yy(-1) * NZ + z
    for d in (1, -1, 2, -2):
        greet(yy(d) * NZ + z, s)
        greet(y * NZ + zz(d), s)
    for d in range(1, NS):
        greet(i, lax.rem(s + d, NS))
    pl.semaphore_wait(barrier, 8 + NS - 1)

    def tell(stage):
        for side, step in ((0, 2 << stage), (1, -(2 << stage))):
            pl.semaphore_signal(
                known.at[stage, side], inc=1, device_id=(y * NZ + zz(step), s), device_id_type=MESH
            )
            if stage == 0:
                pl.semaphore_signal(
                    along.at[side], inc=1, device_id=(yy(step) * NZ + z, s), device_id_type=MESH
                )

    def hear(stage):
        for side in range(2):
            pl.semaphore_wait(known.at[stage, side], 1)
            if stage == 0:
                pl.semaphore_wait(along.at[side], 1)

    wide = pl.ds(NARROW, g_ref.shape[-1] - NARROW)

    def stretch(j):
        return lax.rem(z // 3 + (2, 1, 3, 0)[j], PARTS)

    def count(way, j):
        return 4 if (j < PARTS // 2) == (way > 0) else 3

    tables = {1: (rbuf, rsend, rs_sem, rr_sem), -1: (lbuf, lsend, ls_sem, lr_sem)}
    started = []

    def begin(copy):
        copy.start()
        started.append(copy)

    def ring(way, j, t):
        buf, sends, ssem, rsem = tables[way]
        src = g_ref.at[yy(way * count(way, j)), stretch(j), :, :, wide] if t == 0 else sends.at[j, t - 1]
        return remote(src, buf.at[j, t], ssem.at[j, t], rsem.at[j, t], (up if way > 0 else down, s))

    def ring_step(t):
        for j in range(PARTS):
            for way in (1, -1):
                if t >= count(way, j):
                    continue
                if t > 0:
                    buf, sends, _, _ = tables[way]
                    ring(way, j, t - 1).wait_recv()
                    chunk = yy(way * (count(way, j) - t))
                    sends[j, t - 1] = (
                        loc[chunk, stretch(j), :, :, wide].astype(F32) + buf[j, t - 1].astype(F32)
                    ).astype(BF16)
                begin(ring(way, j, t))

    narrow = pl.ds(0, NARROW)
    raw_far, sum_far = ((6, 4, 2), (5, 3)), ((5, 3, 1), (4, 2))

    def sign(h, side):
        return 1 if h == side else -1

    def part(ref, h, chunk):
        return ref.at[pl.ds(4 * h, 4), chunk // 3, lax.rem(chunk, 3), :, narrow]

    def raw(h, side, n):
        to = zz(sign(h, side))
        return remote(
            part(g_ref, h, zz(sign(h, side) * raw_far[side][n])), araw.at[h, side, n],
            as_sem.at[h, side, n], ar_sem.at[h, side, n], (y * NZ + to, s),
        )

    def paired(h, side, n):
        if n == 2 and side == 1:
            to = zz(sign(h, side))
            src = part(g_ref, h, to)
        else:
            to = zz(sign(h, side) * sum_far[side][n])
            src = asum.at[h, side, n]
        return remote(
            src, afin.at[h, side, n], bs_sem.at[h, side, n], br_sem.at[h, side, n], (y * NZ + to, s)
        )

    def pair_step(h, side, n):
        raw(h, side, n).wait_recv()
        to = zz(sign(h, side) * sum_far[side][n])
        asum[h, side, n] = (
            part(loc, h, to)[...].astype(F32) + araw[h, side, n].astype(F32)
        ).astype(BF16)
        begin(paired(h, side, n))

    tell(0)
    ring_step(0)
    for n in range(3):
        for h in range(2):
            for side in range(2):
                if n < len(raw_far[side]):
                    begin(raw(h, side, n))
    for h in range(2):
        begin(paired(h, 1, 2))
    local.wait()
    ring_step(1)
    hear(0)
    tell(1)
    for side, n in ((1, 0), (0, 1), (1, 1), (0, 2)):
        for h in range(2):
            pair_step(h, side, n)
    ring_step(2)
    hear(1)
    for h in range(2):
        pair_step(h, 0, 0)
    ring_step(3)

    def to_row(d):
        to = yy(d)
        return remote(asend.at[to], abuf.at[d], cs_sem.at[d], cr_sem.at[d], (to * NZ + z, s))

    for h in range(2):
        narrow_sum = part(loc, h, z)[...].astype(F32)
        for n in range(3):
            for side in range(2):
                paired(h, side, n).wait_recv()
                narrow_sum = narrow_sum + afin[h, side, n].astype(F32)
        asend[pl.ds(4 * h, 4)] = narrow_sum
    for d in range(1, NY):
        begin(to_row(d))

    def across(j, a):
        to = 3 * stretch(j) + a
        slot = lax.rem(to - z + NZ, NZ)
        return to, remote(
            zsend.at[j, a], zbuf.at[slot], zs_sem.at[j, a], zr_sem.at[slot], (y * NZ + to, s)
        )

    for j in range(PARTS):
        ring(1, j, count(1, j) - 1).wait_recv()
        ring(-1, j, count(-1, j) - 1).wait_recv()
        total = (
            loc[y, stretch(j), :, :, wide].astype(F32)
            + rbuf[j, count(1, j) - 1].astype(F32)
            + lbuf[j, count(-1, j) - 1].astype(F32)
        )
        zsend[j] = total.astype(BF16)
        for a in range(3):
            to, copy = across(j, a)

            @pl.when(z != to)
            def _():
                copy.start()

            @pl.when(z == to)
            def _():
                own[...] = total[a]

    left_rows = asend[y]
    for d in range(1, NY):
        to_row(d).wait_recv()
        left_rows = left_rows + abuf[d]
    right_rows = own[...]
    for d in range(1, NZ):
        remote(zsend.at[0, 0], zbuf.at[d], zs_sem.at[0, 0], zr_sem.at[d], (up, s)).wait_recv()
        right_rows = right_rows + zbuf[d].astype(F32)

    piece[:, 0:NARROW] = left_rows.astype(BF16)
    piece[:, NARROW:] = right_rows.astype(BF16)
    folded = jnp.zeros((16, 128), F32)
    for side_rows in (left_rows, right_rows):
        for k in range(side_rows.shape[1] // 128):
            square = side_rows[:, k * 128 : (k + 1) * 128]
            folded = folded + square * square
    sq[...] = jnp.sum(folded, axis=0, keepdims=True)

    def to_peer(d):
        return remote(sq, peers.at[d], ps_sem.at[d], pr_sem.at[d], (i, lax.rem(s + d, NS)))

    for d in range(1, NS):
        to_peer(d).start()

    def to_root(k, slot):
        return remote(piece, gath.at[slot], gs_sem.at[k], gr_sem, (root_of(block, s, k), s))

    for k in range(SPANS):
        copy = to_root(k, mine)

        @pl.when(i != root_of(block, s, k))
        def _():
            copy.start()

    row_sq = sq[...]
    for d in range(1, NS):
        to_peer(d).wait_recv()
        row_sq = row_sq + peers[d]
    line[...] = row_sq

    def to_column(b, k, slot):
        return remote(
            line, lines.at[slot], ts_sem.at[b, k], tr_sem, (root_of(b, s, k), s)
        )

    for b in range(BLOCKS):
        for k in range(SPANS):
            copy = to_column(b, k, i)

            @pl.when(i != root_of(b, s, k))
            def _():
                copy.start()

    @pl.when(is_root)
    def _():
        gath[mine] = piece[...]
        lines[i] = row_sq
        remote(
            gath.at[pl.ds(0, PER_BLOCK - 1)], gath.at[pl.ds(0, PER_BLOCK - 1)], us_sem.at[0], gr_sem, (up, s)
        ).wait_recv()

        width = 16 * PER_BLOCK
        grad = gath[...].reshape(width, width)
        exact = grad.astype(F32)
        fb = jnp.sum(exact * exact, keepdims=True)
        inverse = jnp.where(fb > 0.0, 1.0 / fb, 0.0)
        n1 = dot(grad, grad, TN) * inverse
        eye = lax.broadcasted_iota(jnp.int32, (width, width), 0) == lax.broadcasted_iota(
            jnp.int32, (width, width), 1
        )
        trace = jnp.where(fb > 0.0, 1.0, 0.0)
        norm2 = jnp.sum(n1 * n1, keepdims=True)
        nb = n1.astype(BF16)
        n2 = dot(nb, nb, NN)
        n3 = dot(nb, n2.astype(BF16), NN)

        first = 5 * block // 2

        def served(k):
            at = lax.rem(NZ - 2 + 2 * lax.rem(s, 2) + 4 * span + lax.rem(k // 4 + 2, 4), NZ)
            m = (first + lax.rem(k, 4)) * NZ + at - block * PER_BLOCK
            return m, jnp.logical_and(jnp.logical_and(m >= 0, m < PER_BLOCK), m != mine)

        for k in range(16):
            pick[k] = gath[lax.rem(served(k)[0] + PER_BLOCK, PER_BLOCK)]

        others = NY * NZ - 1
        remote(
            lines.at[pl.ds(0, others)], lines.at[pl.ds(0, others)], us_sem.at[0], tr_sem, (up, s)
        ).wait_recv()

        sumsq = jnp.sum(jnp.sum(lines[...], axis=0), keepdims=True)
        limit = TARGET_RMS * width * math.sqrt(BLOCKS * NS)
        clip = limit / jnp.sqrt(sumsq)
        kappa = (limit * limit / width) * (fb / sumsq)
        c2 = kappa * kappa * norm2 + (2.0 * RIDGE) * kappa * trace + RIDGE * RIDGE * width
        c = jnp.sqrt(c2)
        start = lax.rsqrt(jnp.sqrt(c))
        coefs = [v * start for v in shifted(kappa / c, RIDGE / c)]

        high = (coefs[4] * n1 + coefs[5] * n2 + coefs[6] * n3).astype(BF16)
        low = coefs[1] * n1 + coefs[2] * n2 + coefs[3] * n3 + jnp.where(eye, coefs[0], 0.0)
        root = (low + dot(n3.astype(BF16), high, NN)).astype(BF16)
        rows = pick[...].reshape(16 * 16, width)
        hidden = (clip * dot(rows, root, NN)).astype(BF16)
        upd[...] = dot(hidden, root, NN).reshape(16, 16, width)

        def from_root(k, m):
            return remote(upd.at[k], land, us_sem.at[k], ur_sem, (block * PER_BLOCK + m, s))

        @pl.loop(0, 16)
        def _(k):
            m, other = served(k)

            @pl.when(other)
            def _():
                from_root(k, m).start()

        out_ref[...] = upd[4 * lax.rem(lax.rem(ahead, 4) + 2, 4) + y - first]

        @pl.loop(0, 16)
        def _(k):
            m, other = served(k)

            @pl.when(other)
            def _():
                from_root(k, m).wait_send()

    for k in range(SPANS):
        copy = to_root(k, mine)

        @pl.when(i != root_of(block, s, k))
        def _():
            copy.wait_send()

    for d in range(1, NS):
        to_peer(d).wait_send()
    for b in range(BLOCKS):
        for k in range(SPANS):
            copy = to_column(b, k, i)

            @pl.when(i != root_of(b, s, k))
            def _():
                copy.wait_send()

    for copy in started:
        copy.wait_send()
    for j in range(PARTS):
        for a in range(3):
            to, copy = across(j, a)

            @pl.when(z != to)
            def _():
                copy.wait_send()

    @pl.when(jnp.logical_not(is_root))
    def _():
        remote(upd.at[0], land, us_sem.at[0], ur_sem, (up, s)).wait_recv()
        out_ref[...] = land[...]


def body(grad_partials):
    width = grad_partials.shape[-1]
    g = grad_partials.reshape(NY, PARTS, 3, 16, width)
    dma = pltpu.SemaphoreType.DMA
    rest = width - NARROW
    out = pl.pallas_call(
        kernel,
        out_shape=jax.ShapeDtypeStruct((16, width), F32),
        in_specs=[pl.BlockSpec(memory_space=pltpu.HBM)],
        out_specs=pl.BlockSpec(memory_space=pltpu.VMEM),
        scratch_shapes=[
            pltpu.VMEM((NY, PARTS, 3, 16, width), BF16),
            pltpu.VMEM((16, 16, width), BF16),
            pltpu.VMEM((PARTS, 4, 3, 16, rest), BF16),
            pltpu.VMEM((PARTS, 4, 3, 16, rest), BF16),
            pltpu.VMEM((PARTS, 3, 3, 16, rest), BF16),
            pltpu.VMEM((PARTS, 3, 3, 16, rest), BF16),
            pltpu.VMEM((PARTS, 3, 16, rest), BF16),
            pltpu.VMEM((16, rest), F32),
            pltpu.VMEM((NZ, 16, rest), BF16),
            pltpu.VMEM((2, 2, 3, 4, 16, NARROW), BF16),
            pltpu.VMEM((2, 2, 3, 4, 16, NARROW), BF16),
            pltpu.VMEM((2, 2, 3, 4, 16, NARROW), BF16),
            pltpu.VMEM((NY, 16, NARROW), F32),
            pltpu.VMEM((NY, 16, NARROW), F32),
            pltpu.VMEM((16, width), BF16),
            pltpu.VMEM((1, 128), F32),
            pltpu.VMEM((PER_BLOCK, 16, width), BF16),
            pltpu.VMEM((NS, 1, 128), F32),
            pltpu.VMEM((1, 128), F32),
            pltpu.VMEM((NY * NZ, 1, 128), F32),
            pltpu.VMEM((16, 16, width), F32),
            pltpu.VMEM((16, width), F32),
            dma,
            dma((PARTS, 4)), dma((PARTS, 4)), dma((PARTS, 4)), dma((PARTS, 4)),
            dma((PARTS, 3)), dma((NZ,)),
            dma((SPANS,)), dma, dma((NS,)), dma((NS,)),
            dma((BLOCKS, SPANS)), dma, dma((16,)), dma,
            pltpu.SemaphoreType.REGULAR((2, 2)),
            pltpu.SemaphoreType.REGULAR((2,)),
            dma((2, 2, 3)), dma((2, 2, 3)), dma((2, 2, 3)), dma((2, 2, 3)), dma((NY,)), dma((NY,)),
        ],
        compiler_params=pltpu.CompilerParams(
            collective_id=0, has_side_effects=True, vmem_limit_bytes=48 * 2**20
        ),
    )(g)
    return out[None]


def solution(mesh):
    placed = (P("dp", "shard", None, None),)
    return jax.shard_map(
        body, mesh=mesh, in_specs=placed, out_specs=P("shard", "dp", None), check_vma=False
    )
```

```python
import functools
import math

import jax
import jax.numpy as jnp
from jax import lax
from jax.experimental import pallas as pl
from jax.experimental.pallas import tpu as pltpu
from jax.sharding import PartitionSpec as P

MESH = pl.DeviceIdType.MESH
NY, NZ, NS = 8, 12, 8
PARTS = 4
NARROW = 128
PER_BLOCK = 32
BLOCKS = 3
SPANS = 3
RIDGE = 0.1
TARGET_RMS = 0.5
F32, BF16 = jnp.float32, jnp.bfloat16


def series():
    coefs = [25.0 / 16.0, -5.0 / 16.0, 0.0, 0.0, 0.0, 0.0, 0.0]
    for power in range(6):
        coefs[power + 1] -= math.comb(5, power) * 5.0 ** (5 - power) * (-1.0) ** power / 4096.0
    return coefs


def shifted(beta, gamma):
    coefs = series()
    out = []
    scale = jnp.ones_like(beta)
    for j in range(7):
        total = jnp.zeros_like(beta)
        for i in range(6, j - 1, -1):
            total = total * gamma + coefs[i] * math.comb(i, j)
        out.append(total * scale)
        scale = scale * beta
    return out


def root_of(block, shard, k):
    row = 1 + 2 * block + block // 2
    return row * NZ + lax.rem(shard, 2) + 4 * k


def dot(a, b, dims):
    return lax.dot_general(a, b, (dims, ((), ())), preferred_element_type=F32)


NN = ((1,), (0,))
TN = ((0,), (0,))


def kernel(
    g_ref, out_ref,
    loc, pick, rbuf, lbuf, rsend, lsend, zsend, own, zbuf, araw, asum, afin, asend, abuf, piece, sq, gath, peers, line, lines, upd, land,
    loc_sem, rs_sem, rr_sem, ls_sem, lr_sem, zs_sem, zr_sem, gs_sem, gr_sem, ps_sem, pr_sem,
    ts_sem, tr_sem, us_sem, ur_sem, known, along,
    as_sem, ar_sem, bs_sem, br_sem, cs_sem, cr_sem,
):
    i = lax.axis_index("dp")
    s = lax.axis_index("shard")
    y, z = i // NZ, lax.rem(i, NZ)
    block, mine = i // PER_BLOCK, lax.rem(i, PER_BLOCK)
    ahead = lax.rem(z + NZ + 1 - lax.rem(s, 2), NZ)
    span = ahead // 4
    is_root = functools.reduce(jnp.logical_or, [i == root_of(block, s, k) for k in range(SPANS)])

    def yy(d):
        return lax.rem(y + d + NY, NY)

    def zz(d):
        return lax.rem(z + d + NZ, NZ)

    def remote(src, dst, ssem, rsem, dev):
        return pltpu.make_async_remote_copy(
            src_ref=src, dst_ref=dst, send_sem=ssem, recv_sem=rsem,
            device_id=dev, device_id_type=MESH,
        )

    local = pltpu.make_async_copy(g_ref, loc, loc_sem)
    local.start()

    barrier = pltpu.get_barrier_semaphore()

    def greet(dp, shard):
        pl.semaphore_signal(barrier, inc=1, device_id=(dp, shard), device_id_type=MESH)

    up, down = yy(1) * NZ + z, yy(-1) * NZ + z
    for d in (1, -1, 2, -2):
        greet(yy(d) * NZ + z, s)
        greet(y * NZ + zz(d), s)
    for d in range(1, NS):
        greet(i, lax.rem(s + d, NS))
    pl.semaphore_wait(barrier, 8 + NS - 1)

    def tell(stage):
        for side, step in ((0, 2 << stage), (1, -(2 << stage))):
            pl.semaphore_signal(
                known.at[stage, side], inc=1, device_id=(y * NZ + zz(step), s), device_id_type=MESH
            )
            if stage == 0:
                pl.semaphore_signal(
                    along.at[side], inc=1, device_id=(yy(step) * NZ + z, s), device_id_type=MESH
                )

    def hear(stage):
        for side in range(2):
            pl.semaphore_wait(known.at[stage, side], 1)
            if stage == 0:
                pl.semaphore_wait(along.at[side], 1)

    wide = pl.ds(NARROW, g_ref.shape[-1] - NARROW)

    def stretch(j):
        return lax.rem(z // 3 + (2, 1, 3, 0)[j], PARTS)

    def count(way, j):
        return 4 if (j < PARTS // 2) == (way > 0) else 3

    tables = {1: (rbuf, rsend, rs_sem, rr_sem), -1: (lbuf, lsend, ls_sem, lr_sem)}
    started = []

    def begin(copy):
        copy.start()
        started.append(copy)

    def ring(way, j, t):
        buf, sends, ssem, rsem = tables[way]
        src = g_ref.at[yy(way * count(way, j)), stretch(j), :, :, wide] if t == 0 else sends.at[j, t - 1]
        return remote(src, buf.at[j, t], ssem.at[j, t], rsem.at[j, t], (up if way > 0 else down, s))

    def ring_step(t):
        for j in range(PARTS):
            for way in (1, -1):
                if t >= count(way, j):
                    continue
                if t > 0:
                    buf, sends, _, _ = tables[way]
                    ring(way, j, t - 1).wait_recv()
                    chunk = yy(way * (count(way, j) - t))
                    sends[j, t - 1] = (
                        loc[chunk, stretch(j), :, :, wide].astype(F32) + buf[j, t - 1].astype(F32)
                    ).astype(BF16)
                begin(ring(way, j, t))

    narrow = pl.ds(0, NARROW)
    raw_far, sum_far = ((6, 4, 2), (5, 3)), ((5, 3, 1), (4, 2))

    def sign(h, side):
        return 1 if h == side else -1

    def part(ref, h, chunk):
        return ref.at[pl.ds(4 * h, 4), chunk // 3, lax.rem(chunk, 3), :, narrow]

    def raw(h, side, n):
        to = zz(sign(h, side))
        return remote(
            part(g_ref, h, zz(sign(h, side) * raw_far[side][n])), araw.at[h, side, n],
            as_sem.at[h, side, n], ar_sem.at[h, side, n], (y * NZ + to, s),
        )

    def paired(h, side, n):
        if n == 2 and side == 1:
            to = zz(sign(h, side))
            src = part(g_ref, h, to)
        else:
            to = zz(sign(h, side) * sum_far[side][n])
            src = asum.at[h, side, n]
        return remote(
            src, afin.at[h, side, n], bs_sem.at[h, side, n], br_sem.at[h, side, n], (y * NZ + to, s)
        )

    def pair_step(h, side, n):
        raw(h, side, n).wait_recv()
        to = zz(sign(h, side) * sum_far[side][n])
        asum[h, side, n] = (
            part(loc, h, to)[...].astype(F32) + araw[h, side, n].astype(F32)
        ).astype(BF16)
        begin(paired(h, side, n))

    tell(0)
    ring_step(0)
    for n in range(3):
        for h in range(2):
            for side in range(2):
                if n < len(raw_far[side]):
                    begin(raw(h, side, n))
    for h in range(2):
        begin(paired(h, 1, 2))
    local.wait()
    ring_step(1)
    hear(0)
    tell(1)
    for side, n in ((1, 0), (0, 1), (1, 1), (0, 2)):
        for h in range(2):
            pair_step(h, side, n)
    ring_step(2)
    hear(1)
    for h in range(2):
        pair_step(h, 0, 0)
    ring_step(3)

    def to_row(d):
        to = yy(d)
        return remote(asend.at[to], abuf.at[d], cs_sem.at[d], cr_sem.at[d], (to * NZ + z, s))

    for h in range(2):
        narrow_sum = part(loc, h, z)[...].astype(F32)
        for n in range(3):
            for side in range(2):
                paired(h, side, n).wait_recv()
                narrow_sum = narrow_sum + afin[h, side, n].astype(F32)
        asend[pl.ds(4 * h, 4)] = narrow_sum
    for d in range(1, NY):
        begin(to_row(d))

    def across(j, a):
        to = 3 * stretch(j) + a
        slot = lax.rem(to - z + NZ, NZ)
        return to, remote(
            zsend.at[j, a], zbuf.at[slot], zs_sem.at[j, a], zr_sem.at[slot], (y * NZ + to, s)
        )

    for j in range(PARTS):
        ring(1, j, count(1, j) - 1).wait_recv()
        ring(-1, j, count(-1, j) - 1).wait_recv()
        total = (
            loc[y, stretch(j), :, :, wide].astype(F32)
            + rbuf[j, count(1, j) - 1].astype(F32)
            + lbuf[j, count(-1, j) - 1].astype(F32)
        )
        zsend[j] = total.astype(BF16)
        for a in range(3):
            to, copy = across(j, a)

            @pl.when(z != to)
            def _():
                copy.start()

            @pl.when(z == to)
            def _():
                own[...] = total[a]

    left_rows = asend[y]
    for d in range(1, NY):
        to_row(d).wait_recv()
        left_rows = left_rows + abuf[d]
    right_rows = own[...]
    for d in range(1, NZ):
        remote(zsend.at[0, 0], zbuf.at[d], zs_sem.at[0, 0], zr_sem.at[d], (up, s)).wait_recv()
        right_rows = right_rows + zbuf[d].astype(F32)

    piece[:, 0:NARROW] = left_rows.astype(BF16)
    piece[:, NARROW:] = right_rows.astype(BF16)
    folded = jnp.zeros((16, 128), F32)
    for side_rows in (left_rows, right_rows):
        for k in range(side_rows.shape[1] // 128):
            square = side_rows[:, k * 128 : (k + 1) * 128]
            folded = folded + square * square
    sq[...] = jnp.sum(folded, axis=0, keepdims=True)

    def to_peer(d):
        return remote(sq, peers.at[d], ps_sem.at[d], pr_sem.at[d], (i, lax.rem(s + d, NS)))

    for d in range(1, NS):
        to_peer(d).start()

    def to_root(k, slot):
        return remote(piece, gath.at[slot], gs_sem.at[k], gr_sem, (root_of(block, s, k), s))

    for k in range(SPANS):
        copy = to_root(k, mine)

        @pl.when(i != root_of(block, s, k))
        def _():
            copy.start()

    row_sq = sq[...]
    for d in range(1, NS):
        to_peer(d).wait_recv()
        row_sq = row_sq + peers[d]
    line[...] = row_sq

    def to_column(b, k, slot):
        return remote(
            line, lines.at[slot], ts_sem.at[b, k], tr_sem, (root_of(b, s, k), s)
        )

    for b in range(BLOCKS):
        for k in range(SPANS):
            copy = to_column(b, k, i)

            @pl.when(i != root_of(b, s, k))
            def _():
                copy.start()

    @pl.when(is_root)
    def _():
        gath[mine] = piece[...]
        lines[i] = row_sq
        remote(
            gath.at[pl.ds(0, PER_BLOCK - 1)], gath.at[pl.ds(0, PER_BLOCK - 1)], us_sem.at[0], gr_sem, (up, s)
        ).wait_recv()

        width = 16 * PER_BLOCK
        grad = gath[...].reshape(width, width)
        exact = grad.astype(F32)
        fb = jnp.sum(exact * exact, keepdims=True)
        inverse = jnp.where(fb > 0.0, 1.0 / fb, 0.0)
        n1 = dot(grad, grad, TN) * inverse
        eye = lax.broadcasted_iota(jnp.int32, (width, width), 0) == lax.broadcasted_iota(
            jnp.int32, (width, width), 1
        )
        trace = jnp.where(fb > 0.0, 1.0, 0.0)
        norm2 = jnp.sum(n1 * n1, keepdims=True)
        nb = n1.astype(BF16)
        n2 = dot(nb, nb, NN)
        n3 = dot(nb, n2.astype(BF16), NN)

        first = 5 * block // 2

        def served(k):
            turn = lax.rem(k // 4 + 1 - lax.rem(s, 2), 4)
            at = lax.rem(NZ - 1 + lax.rem(s, 2) + 4 * span + turn, NZ)
            m = (first + lax.rem(k, 4)) * NZ + at - block * PER_BLOCK
            return m, jnp.logical_and(jnp.logical_and(m >= 0, m < PER_BLOCK), m != mine)

        for k in range(16):
            pick[k] = gath[lax.rem(served(k)[0] + PER_BLOCK, PER_BLOCK)]

        others = NY * NZ - 1
        remote(
            lines.at[pl.ds(0, others)], lines.at[pl.ds(0, others)], us_sem.at[0], tr_sem, (up, s)
        ).wait_recv()

        sumsq = jnp.sum(jnp.sum(lines[...], axis=0), keepdims=True)
        limit = TARGET_RMS * width * math.sqrt(BLOCKS * NS)
        clip = limit / jnp.sqrt(sumsq)
        kappa = (limit * limit / width) * (fb / sumsq)
        c2 = kappa * kappa * norm2 + (2.0 * RIDGE) * kappa * trace + RIDGE * RIDGE * width
        c = jnp.sqrt(c2)
        start = lax.rsqrt(jnp.sqrt(c))
        coefs = [v * start for v in shifted(kappa / c, RIDGE / c)]

        high = (coefs[4] * n1 + coefs[5] * n2 + coefs[6] * n3).astype(BF16)
        low = coefs[1] * n1 + coefs[2] * n2 + coefs[3] * n3 + jnp.where(eye, coefs[0], 0.0)
        root = (low + dot(n3.astype(BF16), high, NN)).astype(BF16)
        rows = pick[...].reshape(16 * 16, width)
        hidden = (clip * dot(rows, root, NN)).astype(BF16)
        upd[...] = dot(hidden, root, NN).reshape(16, 16, width)

        def from_root(k, m):
            return remote(upd.at[k], land, us_sem.at[k], ur_sem, (block * PER_BLOCK + m, s))

        @pl.loop(0, 16)
        def _(k):
            m, other = served(k)

            @pl.when(other)
            def _():
                from_root(k, m).start()

        out_ref[...] = upd[4 * lax.rem(lax.rem(ahead, 4) + 3 + lax.rem(s, 2), 4) + y - first]

        @pl.loop(0, 16)
        def _(k):
            m, other = served(k)

            @pl.when(other)
            def _():
                from_root(k, m).wait_send()

    for k in range(SPANS):
        copy = to_root(k, mine)

        @pl.when(i != root_of(block, s, k))
        def _():
            copy.wait_send()

    for d in range(1, NS):
        to_peer(d).wait_send()
    for b in range(BLOCKS):
        for k in range(SPANS):
            copy = to_column(b, k, i)

            @pl.when(i != root_of(b, s, k))
            def _():
                copy.wait_send()

    for copy in started:
        copy.wait_send()
    for j in range(PARTS):
        for a in range(3):
            to, copy = across(j, a)

            @pl.when(z != to)
            def _():
                copy.wait_send()

    @pl.when(jnp.logical_not(is_root))
    def _():
        remote(upd.at[0], land, us_sem.at[0], ur_sem, (up, s)).wait_recv()
        out_ref[...] = land[...]


def body(grad_partials):
    width = grad_partials.shape[-1]
    g = grad_partials.reshape(NY, PARTS, 3, 16, width)
    dma = pltpu.SemaphoreType.DMA
    rest = width - NARROW
    out = pl.pallas_call(
        kernel,
        out_shape=jax.ShapeDtypeStruct((16, width), F32),
        in_specs=[pl.BlockSpec(memory_space=pltpu.HBM)],
        out_specs=pl.BlockSpec(memory_space=pltpu.VMEM),
        scratch_shapes=[
            pltpu.VMEM((NY, PARTS, 3, 16, width), BF16),
            pltpu.VMEM((16, 16, width), BF16),
            pltpu.VMEM((PARTS, 4, 3, 16, rest), BF16),
            pltpu.VMEM((PARTS, 4, 3, 16, rest), BF16),
            pltpu.VMEM((PARTS, 3, 3, 16, rest), BF16),
            pltpu.VMEM((PARTS, 3, 3, 16, rest), BF16),
            pltpu.VMEM((PARTS, 3, 16, rest), BF16),
            pltpu.VMEM((16, rest), F32),
            pltpu.VMEM((NZ, 16, rest), BF16),
            pltpu.VMEM((2, 2, 3, 4, 16, NARROW), BF16),
            pltpu.VMEM((2, 2, 3, 4, 16, NARROW), BF16),
            pltpu.VMEM((2, 2, 3, 4, 16, NARROW), BF16),
            pltpu.VMEM((NY, 16, NARROW), F32),
            pltpu.VMEM((NY, 16, NARROW), F32),
            pltpu.VMEM((16, width), BF16),
            pltpu.VMEM((1, 128), F32),
            pltpu.VMEM((PER_BLOCK, 16, width), BF16),
            pltpu.VMEM((NS, 1, 128), F32),
            pltpu.VMEM((1, 128), F32),
            pltpu.VMEM((NY * NZ, 1, 128), F32),
            pltpu.VMEM((16, 16, width), F32),
            pltpu.VMEM((16, width), F32),
            dma,
            dma((PARTS, 4)), dma((PARTS, 4)), dma((PARTS, 4)), dma((PARTS, 4)),
            dma((PARTS, 3)), dma((NZ,)),
            dma((SPANS,)), dma, dma((NS,)), dma((NS,)),
            dma((BLOCKS, SPANS)), dma, dma((16,)), dma,
            pltpu.SemaphoreType.REGULAR((2, 2)),
            pltpu.SemaphoreType.REGULAR((2,)),
            dma((2, 2, 3)), dma((2, 2, 3)), dma((2, 2, 3)), dma((2, 2, 3)), dma((NY,)), dma((NY,)),
        ],
        compiler_params=pltpu.CompilerParams(
            collective_id=0, has_side_effects=True, vmem_limit_bytes=48 * 2**20
        ),
    )(g)
    return out[None]


def solution(mesh):
    placed = (P("dp", "shard", None, None),)
    return jax.shard_map(
        body, mesh=mesh, in_specs=placed, out_specs=P("shard", "dp", None), check_vma=False
    )
```

```python
import functools
import math

import jax
import jax.numpy as jnp
from jax import lax
from jax.experimental import pallas as pl
from jax.experimental.pallas import tpu as pltpu
from jax.sharding import PartitionSpec as P

MESH = pl.DeviceIdType.MESH
NY, NZ, NS = 8, 12, 8
PARTS = 6
PER = NZ // PARTS
NARROW = 128
PER_BLOCK = 32
BLOCKS = 3
SPANS = 3
RIDGE = 0.1
TARGET_RMS = 0.5
F32, BF16 = jnp.float32, jnp.bfloat16


def series():
    coefs = [25.0 / 16.0, -5.0 / 16.0, 0.0, 0.0, 0.0, 0.0, 0.0]
    for power in range(6):
        coefs[power + 1] -= math.comb(5, power) * 5.0 ** (5 - power) * (-1.0) ** power / 4096.0
    return coefs


def shifted(beta, gamma):
    coefs = series()
    out = []
    scale = jnp.ones_like(beta)
    for j in range(7):
        total = jnp.zeros_like(beta)
        for i in range(6, j - 1, -1):
            total = total * gamma + coefs[i] * math.comb(i, j)
        out.append(total * scale)
        scale = scale * beta
    return out


def root_of(block, shard, k):
    row = 1 + 2 * block + block // 2
    return row * NZ + lax.rem(shard, 2) + 4 * k


def dot(a, b, dims):
    return lax.dot_general(a, b, (dims, ((), ())), preferred_element_type=F32)


NN = ((1,), (0,))
TN = ((0,), (0,))


def kernel(
    g_ref, out_ref,
    loc, pick, rbuf, lbuf, rsend, lsend, zsend, own, zbuf, araw, asum, afin, asend, abuf, piece, sq, gath, peers, line, lines, upd, land,
    loc_sem, rs_sem, rr_sem, ls_sem, lr_sem, zs_sem, zr_sem, gs_sem, gr_sem, ps_sem, pr_sem,
    ts_sem, tr_sem, us_sem, ur_sem, known, along,
    as_sem, ar_sem, bs_sem, br_sem, cs_sem, cr_sem,
):
    i = lax.axis_index("dp")
    s = lax.axis_index("shard")
    y, z = i // NZ, lax.rem(i, NZ)
    block, mine = i // PER_BLOCK, lax.rem(i, PER_BLOCK)
    ahead = lax.rem(z + NZ + 1 - lax.rem(s, 2), NZ)
    span = ahead // 4
    is_root = functools.reduce(jnp.logical_or, [i == root_of(block, s, k) for k in range(SPANS)])

    def yy(d):
        return lax.rem(y + d + NY, NY)

    def zz(d):
        return lax.rem(z + d + NZ, NZ)

    def remote(src, dst, ssem, rsem, dev):
        return pltpu.make_async_remote_copy(
            src_ref=src, dst_ref=dst, send_sem=ssem, recv_sem=rsem,
            device_id=dev, device_id_type=MESH,
        )

    local = pltpu.make_async_copy(g_ref, loc, loc_sem)
    local.start()

    barrier = pltpu.get_barrier_semaphore()

    def greet(dp, shard):
        pl.semaphore_signal(barrier, inc=1, device_id=(dp, shard), device_id_type=MESH)

    up, down = yy(1) * NZ + z, yy(-1) * NZ + z
    for d in (1, -1, 2, -2):
        greet(yy(d) * NZ + z, s)
        greet(y * NZ + zz(d), s)
    for d in range(1, NS):
        greet(i, lax.rem(s + d, NS))
    pl.semaphore_wait(barrier, 8 + NS - 1)

    def tell(stage):
        for side, step in ((0, 2 << stage), (1, -(2 << stage))):
            pl.semaphore_signal(
                known.at[stage, side], inc=1, device_id=(y * NZ + zz(step), s), device_id_type=MESH
            )
            if stage == 0:
                pl.semaphore_signal(
                    along.at[side], inc=1, device_id=(yy(step) * NZ + z, s), device_id_type=MESH
                )

    def hear(stage):
        for side in range(2):
            pl.semaphore_wait(known.at[stage, side], 1)
            if stage == 0:
                pl.semaphore_wait(along.at[side], 1)

    wide = pl.ds(NARROW, g_ref.shape[-1] - NARROW)

    def stretch(j):
        return lax.rem(z // PER + (3, 2, 4, 1, 5, 0)[j], PARTS)

    def count(way, j):
        return 4 if (j < PARTS // 2) == (way > 0) else 3

    tables = {1: (rbuf, rsend, rs_sem, rr_sem), -1: (lbuf, lsend, ls_sem, lr_sem)}
    started = []

    def begin(copy):
        copy.start()
        started.append(copy)

    def ring(way, j, t):
        buf, sends, ssem, rsem = tables[way]
        src = g_ref.at[yy(way * count(way, j)), stretch(j), :, :, wide] if t == 0 else sends.at[j, t - 1]
        return remote(src, buf.at[j, t], ssem.at[j, t], rsem.at[j, t], (up if way > 0 else down, s))

    def ring_step(t):
        for j in range(PARTS):
            for way in (1, -1):
                if t >= count(way, j):
                    continue
                if t > 0:
                    buf, sends, _, _ = tables[way]
                    ring(way, j, t - 1).wait_recv()
                    chunk = yy(way * (count(way, j) - t))
                    sends[j, t - 1] = (
                        loc[chunk, stretch(j), :, :, wide].astype(F32) + buf[j, t - 1].astype(F32)
                    ).astype(BF16)
                begin(ring(way, j, t))

    narrow = pl.ds(0, NARROW)
    raw_far, sum_far = ((6, 4, 2), (5, 3)), ((5, 3, 1), (4, 2))

    def sign(h, side):
        return 1 if h == side else -1

    def part(ref, h, chunk):
        return ref.at[pl.ds(4 * h, 4), chunk // PER, lax.rem(chunk, PER), :, narrow]

    def raw(h, side, n):
        to = zz(sign(h, side))
        return remote(
            part(g_ref, h, zz(sign(h, side) * raw_far[side][n])), araw.at[h, side, n],
            as_sem.at[h, side, n], ar_sem.at[h, side, n], (y * NZ + to, s),
        )

    def paired(h, side, n):
        if n == 2 and side == 1:
            to = zz(sign(h, side))
            src = part(g_ref, h, to)
        else:
            to = zz(sign(h, side) * sum_far[side][n])
            src = asum.at[h, side, n]
        return remote(
            src, afin.at[h, side, n], bs_sem.at[h, side, n], br_sem.at[h, side, n], (y * NZ + to, s)
        )

    def pair_step(h, side, n):
        raw(h, side, n).wait_recv()
        to = zz(sign(h, side) * sum_far[side][n])
        asum[h, side, n] = (
            part(loc, h, to)[...].astype(F32) + araw[h, side, n].astype(F32)
        ).astype(BF16)
        begin(paired(h, side, n))

    tell(0)
    ring_step(0)
    for n in range(3):
        for h in range(2):
            for side in range(2):
                if n < len(raw_far[side]):
                    begin(raw(h, side, n))
    for h in range(2):
        begin(paired(h, 1, 2))
    local.wait()
    ring_step(1)
    hear(0)
    tell(1)
    for side, n in ((1, 0), (0, 1), (1, 1), (0, 2)):
        for h in range(2):
            pair_step(h, side, n)
    ring_step(2)
    hear(1)
    for h in range(2):
        pair_step(h, 0, 0)
    ring_step(3)

    def to_row(d):
        to = yy(d)
        return remote(asend.at[to], abuf.at[d], cs_sem.at[d], cr_sem.at[d], (to * NZ + z, s))

    for h in range(2):
        narrow_sum = part(loc, h, z)[...].astype(F32)
        for n in range(3):
            for side in range(2):
                paired(h, side, n).wait_recv()
                narrow_sum = narrow_sum + afin[h, side, n].astype(F32)
        asend[pl.ds(4 * h, 4)] = narrow_sum
    for d in range(1, NY):
        begin(to_row(d))

    def across(j, a):
        to = PER * stretch(j) + a
        slot = lax.rem(to - z + NZ, NZ)
        return to, remote(
            zsend.at[j, a], zbuf.at[slot], zs_sem.at[j, a], zr_sem.at[slot], (y * NZ + to, s)
        )

    for j in range(PARTS):
        ring(1, j, count(1, j) - 1).wait_recv()
        ring(-1, j, count(-1, j) - 1).wait_recv()
        total = (
            loc[y, stretch(j), :, :, wide].astype(F32)
            + rbuf[j, count(1, j) - 1].astype(F32)
            + lbuf[j, count(-1, j) - 1].astype(F32)
        )
        zsend[j] = total.astype(BF16)
        for a in range(PER):
            to, copy = across(j, a)

            @pl.when(z != to)
            def _():
                copy.start()

            @pl.when(z == to)
            def _():
                own[...] = total[a]

    left_rows = asend[y]
    for d in range(1, NY):
        to_row(d).wait_recv()
        left_rows = left_rows + abuf[d]
    right_rows = own[...]
    for d in range(1, NZ):
        remote(zsend.at[0, 0], zbuf.at[d], zs_sem.at[0, 0], zr_sem.at[d], (up, s)).wait_recv()
        right_rows = right_rows + zbuf[d].astype(F32)

    piece[:, 0:NARROW] = left_rows.astype(BF16)
    piece[:, NARROW:] = right_rows.astype(BF16)
    folded = jnp.zeros((16, 128), F32)
    for side_rows in (left_rows, right_rows):
        for k in range(side_rows.shape[1] // 128):
            square = side_rows[:, k * 128 : (k + 1) * 128]
            folded = folded + square * square
    sq[...] = jnp.sum(folded, axis=0, keepdims=True)

    def to_peer(d):
        return remote(sq, peers.at[d], ps_sem.at[d], pr_sem.at[d], (i, lax.rem(s + d, NS)))

    for d in range(1, NS):
        to_peer(d).start()

    def to_root(k, slot):
        return remote(piece, gath.at[slot], gs_sem.at[k], gr_sem, (root_of(block, s, k), s))

    for k in range(SPANS):
        copy = to_root(k, mine)

        @pl.when(i != root_of(block, s, k))
        def _():
            copy.start()

    row_sq = sq[...]
    for d in range(1, NS):
        to_peer(d).wait_recv()
        row_sq = row_sq + peers[d]
    line[...] = row_sq

    def to_column(b, k, slot):
        return remote(
            line, lines.at[slot], ts_sem.at[b, k], tr_sem, (root_of(b, s, k), s)
        )

    for b in range(BLOCKS):
        for k in range(SPANS):
            copy = to_column(b, k, i)

            @pl.when(i != root_of(b, s, k))
            def _():
                copy.start()

    @pl.when(is_root)
    def _():
        gath[mine] = piece[...]
        lines[i] = row_sq
        remote(
            gath.at[pl.ds(0, PER_BLOCK - 1)], gath.at[pl.ds(0, PER_BLOCK - 1)], us_sem.at[0], gr_sem, (up, s)
        ).wait_recv()

        width = 16 * PER_BLOCK
        grad = gath[...].reshape(width, width)
        exact = grad.astype(F32)
        fb = jnp.sum(exact * exact, keepdims=True)
        inverse = jnp.where(fb > 0.0, 1.0 / fb, 0.0)
        n1 = dot(grad, grad, TN) * inverse
        eye = lax.broadcasted_iota(jnp.int32, (width, width), 0) == lax.broadcasted_iota(
            jnp.int32, (width, width), 1
        )
        trace = jnp.where(fb > 0.0, 1.0, 0.0)
        norm2 = jnp.sum(n1 * n1, keepdims=True)
        nb = n1.astype(BF16)
        n2 = dot(nb, nb, NN)
        n3 = dot(nb, n2.astype(BF16), NN)

        first = 5 * block // 2

        def served(k):
            turn = lax.rem(k // 4 + 1 - lax.rem(s, 2), 4)
            at = lax.rem(NZ - 1 + lax.rem(s, 2) + 4 * span + turn, NZ)
            m = (first + lax.rem(k, 4)) * NZ + at - block * PER_BLOCK
            return m, jnp.logical_and(jnp.logical_and(m >= 0, m < PER_BLOCK), m != mine)

        for k in range(16):
            pick[k] = gath[lax.rem(served(k)[0] + PER_BLOCK, PER_BLOCK)]

        others = NY * NZ - 1
        remote(
            lines.at[pl.ds(0, others)], lines.at[pl.ds(0, others)], us_sem.at[0], tr_sem, (up, s)
        ).wait_recv()

        sumsq = jnp.sum(jnp.sum(lines[...], axis=0), keepdims=True)
        limit = TARGET_RMS * width * math.sqrt(BLOCKS * NS)
        clip = limit / jnp.sqrt(sumsq)
        kappa = (limit * limit / width) * (fb / sumsq)
        c2 = kappa * kappa * norm2 + (2.0 * RIDGE) * kappa * trace + RIDGE * RIDGE * width
        c = jnp.sqrt(c2)
        start = lax.rsqrt(jnp.sqrt(c))
        coefs = [v * start for v in shifted(kappa / c, RIDGE / c)]

        high = (coefs[4] * n1 + coefs[5] * n2 + coefs[6] * n3).astype(BF16)
        low = coefs[1] * n1 + coefs[2] * n2 + coefs[3] * n3 + jnp.where(eye, coefs[0], 0.0)
        root = (low + dot(n3.astype(BF16), high, NN)).astype(BF16)
        rows = pick[...].reshape(16 * 16, width)
        hidden = (clip * dot(rows, root, NN)).astype(BF16)
        upd[...] = dot(hidden, root, NN).reshape(16, 16, width)

        def from_root(k, m):
            return remote(upd.at[k], land, us_sem.at[k], ur_sem, (block * PER_BLOCK + m, s))

        @pl.loop(0, 16)
        def _(k):
            m, other = served(k)

            @pl.when(other)
            def _():
                from_root(k, m).start()

        out_ref[...] = upd[4 * lax.rem(lax.rem(ahead, 4) + 3 + lax.rem(s, 2), 4) + y - first]

        @pl.loop(0, 16)
        def _(k):
            m, other = served(k)

            @pl.when(other)
            def _():
                from_root(k, m).wait_send()

    for k in range(SPANS):
        copy = to_root(k, mine)

        @pl.when(i != root_of(block, s, k))
        def _():
            copy.wait_send()

    for d in range(1, NS):
        to_peer(d).wait_send()
    for b in range(BLOCKS):
        for k in range(SPANS):
            copy = to_column(b, k, i)

            @pl.when(i != root_of(b, s, k))
            def _():
                copy.wait_send()

    for copy in started:
        copy.wait_send()
    for j in range(PARTS):
        for a in range(PER):
            to, copy = across(j, a)

            @pl.when(z != to)
            def _():
                copy.wait_send()

    @pl.when(jnp.logical_not(is_root))
    def _():
        remote(upd.at[0], land, us_sem.at[0], ur_sem, (up, s)).wait_recv()
        out_ref[...] = land[...]


def body(grad_partials):
    width = grad_partials.shape[-1]
    g = grad_partials.reshape(NY, PARTS, PER, 16, width)
    dma = pltpu.SemaphoreType.DMA
    rest = width - NARROW
    out = pl.pallas_call(
        kernel,
        out_shape=jax.ShapeDtypeStruct((16, width), F32),
        in_specs=[pl.BlockSpec(memory_space=pltpu.HBM)],
        out_specs=pl.BlockSpec(memory_space=pltpu.VMEM),
        scratch_shapes=[
            pltpu.VMEM((NY, PARTS, PER, 16, width), BF16),
            pltpu.VMEM((16, 16, width), BF16),
            pltpu.VMEM((PARTS, 4, PER, 16, rest), BF16),
            pltpu.VMEM((PARTS, 4, PER, 16, rest), BF16),
            pltpu.VMEM((PARTS, 3, PER, 16, rest), BF16),
            pltpu.VMEM((PARTS, 3, PER, 16, rest), BF16),
            pltpu.VMEM((PARTS, PER, 16, rest), BF16),
            pltpu.VMEM((16, rest), F32),
            pltpu.VMEM((NZ, 16, rest), BF16),
            pltpu.VMEM((2, 2, 3, 4, 16, NARROW), BF16),
            pltpu.VMEM((2, 2, 3, 4, 16, NARROW), BF16),
            pltpu.VMEM((2, 2, 3, 4, 16, NARROW), BF16),
            pltpu.VMEM((NY, 16, NARROW), F32),
            pltpu.VMEM((NY, 16, NARROW), F32),
            pltpu.VMEM((16, width), BF16),
            pltpu.VMEM((1, 128), F32),
            pltpu.VMEM((PER_BLOCK, 16, width), BF16),
            pltpu.VMEM((NS, 1, 128), F32),
            pltpu.VMEM((1, 128), F32),
            pltpu.VMEM((NY * NZ, 1, 128), F32),
            pltpu.VMEM((16, 16, width), F32),
            pltpu.VMEM((16, width), F32),
            dma,
            dma((PARTS, 4)), dma((PARTS, 4)), dma((PARTS, 4)), dma((PARTS, 4)),
            dma((PARTS, PER)), dma((NZ,)),
            dma((SPANS,)), dma, dma((NS,)), dma((NS,)),
            dma((BLOCKS, SPANS)), dma, dma((16,)), dma,
            pltpu.SemaphoreType.REGULAR((2, 2)),
            pltpu.SemaphoreType.REGULAR((2,)),
            dma((2, 2, 3)), dma((2, 2, 3)), dma((2, 2, 3)), dma((2, 2, 3)), dma((NY,)), dma((NY,)),
        ],
        compiler_params=pltpu.CompilerParams(
            collective_id=0, has_side_effects=True, vmem_limit_bytes=48 * 2**20
        ),
    )(g)
    return out[None]


def solution(mesh):
    placed = (P("dp", "shard", None, None),)
    return jax.shard_map(
        body, mesh=mesh, in_specs=placed, out_specs=P("shard", "dp", None), check_vma=False
    )
```
